256 devices in a mesh: dp: 16 (over z_lo, x), sp: 16 (over z_hi, y, core).
Axes of the slice: x: 4, y: 4, z: 8 (z_hi: 2, z_lo: 4; z = z_hi * 4 + z_lo), core: 2. Of those that a mesh axis runs over, the one named last changes fastest.
Arguments:
- queries: bfloat16 [2, 16, 2048, 2048], P(None, 'dp', 'sp'), may hold values from -40 to 40
- dout: bfloat16 [2, 16, 2048, 2048], P(None, 'dp', 'sp'), may hold values from -16 to 16
- keys: bfloat16 [16, 2048, 1024], P('dp', 'sp'), may hold values from -40 to 40
- values: bfloat16 [16, 2048, 1024], P('dp', 'sp'), may hold values from -6 to 6
- gain: float32 [2, 128], replicated, may hold values from 0.5 to 2
- segments: int32 [16, 2048], P('dp', 'sp'), may hold values from 0 to 7, never falling along the last dimension, each value on 1 to 1024 neighbouring positions
Outputs:
- dqueries: bfloat16 [2, 16, 2048, 2048], P(None, 'dp', 'sp')
- dkeys: bfloat16 [16, 2048, 1024], P('dp', 'sp')
- dvalues: bfloat16 [16, 2048, 1024], P('dp', 'sp')
- dgain: float32 [2, 128], replicated
The draws below stay inside these ranges and needn't reach their ends.
All inputs are finite; a program needn't handle non-finite values.
Results may differ from the reference program's by a relative error of at most 0.01.
The reference program's roundings to bfloat16 on the way count: a program that leaves them out, or rounds other values in their place, can miss the bound.
Values may be sent and summed in bfloat16 or wider, within the bound.
No kernel may reach another device: no remote copies, remote signals or barrier semaphores. Data moves between devices by JAX's collectives and lax.ppermute only.
A program may use at most 64 MiB of HBM per device.

```python
import math
import jax
import jax.numpy as jnp
import numpy as np
from jax import lax

H = 16
KV = 8
HD = 128
LAYERS = 2
L = 2048
SEQS = 16
N_SP = 16


def draw_keys(key, part):
    key = jax.random.fold_in(key, 3)
    first = jax.random.fold_in(key, 0)
    out = jnp.clip(jax.random.normal(first, (SEQS, L, KV, HD), jnp.float32), -6.0, 6.0)
    return out.reshape(SEQS, L, KV * HD).astype(jnp.bfloat16)


def draw_queries(key, part):
    key = jax.random.fold_in(key, 5)
    first, second = jax.random.split(key, 2)
    spread = jnp.exp(jax.random.uniform(second, (LAYERS, SEQS, L, H, 1), jnp.float32, 0.0, math.log(10.0)))
    out = jnp.clip(jax.random.normal(first, (LAYERS, SEQS, L, H, HD), jnp.float32), -4.0, 4.0) * spread
    return out.reshape(LAYERS, SEQS, L, H * HD).astype(jnp.bfloat16)


def draw_dout(key, part):
    key = jax.random.fold_in(key, 7)
    ramp_seq = 0.6 + 1.2 * jnp.arange(SEQS, dtype=jnp.float32) / SEQS
    ramp_tok = 0.6 + 1.2 * jnp.arange(L, dtype=jnp.float32) / L
    ramp = ramp_seq[None, :, None, None] * ramp_tok[None, None, :, None]
    out = jnp.clip(jax.random.normal(key, (LAYERS, SEQS, L, H * HD), jnp.float32), -4.0, 4.0) * ramp
    return out.astype(jnp.bfloat16)


def levels(rng, shape, cuts, least, top_value):
    loudness, own = 1.0, jax.random.fold_in(rng, 6)
    for axis_at, blocks in cuts:
        steps = jnp.exp(jax.random.uniform(jax.random.fold_in(own, axis_at), (blocks,), jnp.float32, least / len(cuts), top_value / len(cuts)))
        loudness = loudness * jnp.repeat(steps, shape[axis_at] // blocks).reshape([-1 if axis == axis_at else 1 for axis in range(len(shape))])
    return loudness


def split_up(count, total, most, lean):
    weights = [(1 << 20) // math.isqrt(standing ** lean) + 1 for standing in range(2, count + 1)]
    rest, counts = total - most - (count - 1), [1] * (count - 1)
    while rest > 0:
        candidates = [i for i in range(count - 1) if counts[i] < most]
        pool, remaining = sum([weights[i] for i in candidates]), rest
        for i in candidates:
            extra = min(most - counts[i], max(1, remaining * weights[i] // pool), rest)
            counts[i] = counts[i] + extra
            rest = rest - extra
    return np.array([most] + counts)


def uneven_parts(stream_key, amount, total, reach, skew):
    if amount == 2:
        one = jax.random.randint(stream_key, (), max(1, total - reach), min(reach, total - 1) + 1)
        return jnp.stack([one, total - one])
    tallies = jnp.asarray(split_up(amount, total, reach, skew), jnp.int32)
    couples = (amount - 1) // 2
    source_of, receiver = tallies[1:1 + 2 * couples:2], tallies[2:2 + 2 * couples:2]
    slack = jnp.minimum(source_of - 1, reach - receiver)
    moved = jax.random.randint(jax.random.fold_in(stream_key, 1), (couples,), 0, 1 << 20) % (slack + 1)
    tallies = tallies.at[1:1 + 2 * couples:2].set(source_of - moved).at[2:2 + 2 * couples:2].set(receiver + moved)
    return tallies[jax.random.permutation(jax.random.fold_in(stream_key, 2), amount)]


def noise(key, shape, width, limit, cuts=(), kind=jnp.bfloat16):
    result = jax.random.normal(key, shape, jnp.float32) * width
    if len(cuts) > 0:
        result = levels(key, shape, cuts, -0.22, 0.18) * result
    return jnp.clip(result, min=-limit, max=limit).astype(kind)


def setup_inputs(seed: int = 0) -> dict:
    arg_keys = jax.random.split(jax.random.key(seed), 7)
    queries = draw_queries(jax.random.fold_in(arg_keys[6], 71), 0)
    dout = draw_dout(jax.random.fold_in(arg_keys[6], 71), 0)
    keys = draw_keys(jax.random.fold_in(arg_keys[6], 71), 0)
    values = noise(arg_keys[3], (SEQS, L, KV * HD), 1.0, 6.0, ((0, 16), (1, 16)))
    gain = jnp.clip(jnp.exp(jax.random.uniform(arg_keys[4], (LAYERS, HD), jnp.float32, math.log(0.5), math.log(2.0))), 0.5, 2.0)
    segments = jax.vmap(lambda own: jnp.searchsorted(jnp.cumsum(uneven_parts(own, max(3, L // 256), L, L // 2, 1)), jnp.arange(L), side="right"))(jax.random.split(arg_keys[5], SEQS)).reshape((SEQS, L)).astype(jnp.int32)
    return {"queries": queries, "dout": dout, "keys": keys, "values": values, "gain": gain, "segments": segments}


def block_grads(query_blk, dout_blk, seg_q, pos_q, key_h, value_h, seg_k, pos_k, gain_l, scale):
    qf = query_blk.astype(jnp.float32)
    inv = lax.rsqrt(lax.optimization_barrier(jnp.mean(qf * qf, axis=-1, keepdims=True)) + 1e-06)
    qhat = qf * inv
    normed = (qhat * gain_l).astype(jnp.bfloat16)
    nf = normed.astype(jnp.float32)
    kf = key_h.astype(jnp.float32)
    vf = value_h.astype(jnp.float32)
    df = dout_blk.astype(jnp.float32)
    scores = jnp.einsum('bkgd,skd->kgbs', nf, kf) * scale
    allowed = (seg_q[:, None] == seg_k[None, :]) & (pos_k[None, :] <= pos_q[:, None])
    scores = jnp.where(allowed, scores, -1e+30)
    top = lax.optimization_barrier(jnp.max(scores, axis=-1, keepdims=True))
    expo = jnp.exp(scores - top)
    prob = expo / lax.optimization_barrier(jnp.sum(expo, axis=-1, keepdims=True))
    dprob = jnp.einsum('bkgd,skd->kgbs', df, vf)
    delta = lax.optimization_barrier(jnp.sum(prob * dprob, axis=-1, keepdims=True))
    dscore = (prob * (dprob - delta) * scale).astype(jnp.bfloat16).astype(jnp.float32)
    prob16 = prob.astype(jnp.bfloat16).astype(jnp.float32)
    dvalue = jnp.einsum('kgbs,bkgd->skgd', prob16, df)
    dkey = jnp.einsum('kgbs,bkgd->skgd', dscore, nf)
    dnorm = jnp.einsum('kgbs,skd->bkgd', dscore, kf)
    dgain = lax.optimization_barrier(jnp.sum(dnorm * qhat, axis=(0, 1, 2)))
    scaled = dnorm * gain_l
    dquery = inv * (scaled - qhat * lax.optimization_barrier(jnp.mean(scaled * qhat, axis=-1, keepdims=True)))
    return (dquery.astype(jnp.bfloat16), dkey, dvalue, dgain)

def fold_copies(total, group, copies):
    partial_sum = lax.optimization_barrier(jnp.sum(total.reshape(L, KV, copies, group // copies, HD), axis=3)).astype(jnp.bfloat16)
    partial_sum = lax.optimization_barrier(partial_sum)
    whole = lax.optimization_barrier(jnp.sum(partial_sum.astype(jnp.float32), axis=2))
    return whole.astype(jnp.bfloat16).reshape(L, KV * HD)

def reference(queries, dout, keys, values, gain, segments):
    scale = 1.0 / math.sqrt(HD)
    group = H // KV
    copies = max(1, N_SP // KV)
    block = min(512, L)
    count = L // block
    positions = jnp.arange(L, dtype=jnp.int32)

    def one_sequence(items):
        query_s, dout_s, key_s, value_s, seg = items
        key_h = key_s.reshape(L, KV, HD)
        value_h = value_s.reshape(L, KV, HD)
        dkey_total = jnp.zeros((L, KV, group, HD), jnp.float32)
        dvalue_total = jnp.zeros((L, KV, group, HD), jnp.float32)
        dq_list = []
        dg_list = []
        for layer in range(LAYERS):
            query_b = query_s[layer].reshape(count, block, KV, group, HD)
            dout_b = dout_s[layer].reshape(count, block, KV, group, HD)
            seg_b = seg.reshape(count, block)
            pos_b = positions.reshape(count, block)

            def step(carry, xs):
                dk_acc, dv_acc, dg_acc = carry
                dq, dk, dv, dg = block_grads(xs[0], xs[1], xs[2], xs[3], key_h, value_h, seg, positions, gain[layer], scale)
                return ((dk_acc + dk, dv_acc + dv, dg_acc + dg), dq)
            init = (jnp.zeros((L, KV, group, HD), jnp.float32), jnp.zeros((L, KV, group, HD), jnp.float32), jnp.zeros((HD,), jnp.float32))
            (dk_l, dv_l, dg_l), dq_l = lax.scan(step, init, (query_b, dout_b, seg_b, pos_b))
            dkey_total = dkey_total + dk_l
            dvalue_total = dvalue_total + dv_l
            dq_list.append(dq_l.reshape(L, H * HD))
            dg_list.append(dg_l)
        return (jnp.stack(dq_list), fold_copies(dkey_total, group, copies), fold_copies(dvalue_total, group, copies), jnp.stack(dg_list))
    dq, dkeys, dvalues, dgains = lax.map(one_sequence, (jnp.transpose(queries, (1, 0, 2, 3)), jnp.transpose(dout, (1, 0, 2, 3)), keys, values, segments))
    return (jnp.transpose(dq, (1, 0, 2, 3)), dkeys, dvalues, lax.optimization_barrier(jnp.sum(dgains, axis=0)))
```

```python
import functools
import math

import jax
import jax.numpy as jnp
from jax import lax
from jax.experimental import pallas as pl
from jax.experimental.pallas import tpu as pltpu
from jax.sharding import PartitionSpec as P

F32 = jnp.float32
BF16 = jnp.bfloat16
HD = 128
IDS = 16
NT = (((1,), (1,)), ((), ()))
NN = (((1,), (0,)), ((), ()))


def params(mib):
    return pltpu.CompilerParams(vmem_limit_bytes=mib << 20)


def whole():
    return pl.BlockSpec(memory_space=pltpu.VMEM)


def pack_kv_kernel(key_ref, value_ref, seg_ref, out_ref):
    parts, _, width = out_ref.shape
    rows = key_ref.shape[0]
    ids = jnp.broadcast_to(seg_ref[...].astype(F32), (IDS, rows)).astype(BF16)
    for h in range(parts):
        cols = slice(h * width, (h + 1) * width)
        out_ref[h, :rows, :] = key_ref[:, cols]
        out_ref[h, rows : 2 * rows, :] = value_ref[:, cols]
        out_ref[h, 2 * rows :, :] = ids


def pack_q_kernel(query_ref, dout_ref, out_ref):
    parts, twice, _, width = out_ref.shape
    layers = twice // 2
    for h in range(parts):
        cols = slice(h * width, (h + 1) * width)
        for layer in range(layers):
            out_ref[h, layer] = query_ref[layer, :, cols]
            out_ref[h, layers + layer] = dout_ref[layer, :, cols]


def unpack_q_kernel(in_ref, out_ref):
    parts, layers, _, width = in_ref.shape
    for h in range(parts):
        for layer in range(layers):
            out_ref[layer, :, h * width : (h + 1) * width] = in_ref[h, layer]


def combine_kernel(own_ref, cross_ref, out_ref):
    out_ref[...] = (own_ref[...] + cross_ref[...].astype(F32)).astype(BF16)


def unpack_kv_kernel(in_ref, dk_ref, dv_ref):
    parts, twice, width = in_ref.shape
    rows = twice // 2
    for h in range(parts):
        cols = slice(h * width, (h + 1) * width)
        dk_ref[:, cols] = in_ref[h, :rows, :]
        dv_ref[:, cols] = in_ref[h, rows:, :]


def attention_kernel(
    upper_ref,
    own_kv_ref,
    low_kv_ref,
    qd_ref,
    gain_ref,
    dq_ref,
    own_ref,
    cross_ref,
    dgain_ref,
    k_all,
    v_all,
    kt_all,
    start_all,
    normed,
    dout,
    score,
    dprob,
    acc,
    dqt,
):
    blocks, layers, rows, width = dq_ref.shape
    group = width // HD
    size = 2 * rows
    half = blocks // 2
    stack = layers * group * size
    scale = 1.0 / math.sqrt(HD)
    upper = upper_ref[0] > 0

    for side, ref in enumerate((low_kv_ref, own_kv_ref)):
        for b in range(half):
            at = side * half + b
            for j in range(2):
                part = slice(j * rows, (j + 1) * rows)
                kt = ref[2 * b + j, :rows, :]
                k_all[at, part, :] = kt
                v_all[at, part, :] = ref[2 * b + j, rows : 2 * rows, :]
                kt_all[at, :, part] = kt.astype(F32).T.astype(BF16)

    ids_own = jnp.concatenate(
        [own_kv_ref[b, 2 * rows :, :][:1].astype(F32) for b in range(blocks)], 0
    )
    ids_low = jnp.concatenate(
        [low_kv_ref[b, 2 * rows :, :][:1].astype(F32) for b in range(blocks)], 0
    )
    begin = jnp.zeros((blocks, rows), F32)
    for doc in range(8):
        below = jnp.sum((ids_own < doc).astype(F32), keepdims=True)
        below_low = jnp.sum((ids_low < doc).astype(F32), keepdims=True)
        total = below + jnp.where(upper, below_low, float(blocks * rows))
        begin = jnp.where(ids_own == doc, total, begin)
    for b in range(half):
        start_all[b] = jnp.concatenate([begin[2 * b : 2 * b + 1], begin[2 * b + 1 : 2 * b + 2]], 1)

    acc[...] = jnp.zeros_like(acc)
    dgain_ref[...] = jnp.zeros_like(dgain_ref)

    def part_of(i, layer, h, offset):
        cols = slice(h * HD, (h + 1) * HD)
        return jnp.concatenate(
            [qd_ref[2 * i + j, offset + layer, :, cols] for j in range(2)], 0
        )

    def norm_of(i, layer, h):
        q = part_of(i, layer, h, 0).astype(F32)
        inv = lax.rsqrt(jnp.mean(q * q, axis=-1, keepdims=True) + 1e-6)
        return q * inv, inv

    def q_block(i, carry):
        for h in range(group):
            for layer in range(layers):
                at = slice((h * layers + layer) * size, (h * layers + layer + 1) * size)
                qhat, _ = norm_of(i, layer, h)
                normed[at, :] = (qhat * gain_ref[layer : layer + 1, :]).astype(BF16)
                dout[at, :] = part_of(i, layer, h, layers)
        begin_row = start_all[i]
        first = jnp.min(begin_row).astype(jnp.int32) // size
        last = half + i
        count = last - first + 1
        begin_all = jnp.concatenate([begin_row] * (layers * group), 1).astype(jnp.int32)
        token = last * size + lax.broadcasted_iota(jnp.int32, (1, size), 1)
        token_all = jnp.concatenate([token] * (layers * group), 1)

        def scores(j, top):
            kb = first + j
            s = lax.dot_general(k_all[kb], normed[...], NT, preferred_element_type=F32)
            u = kb * size + lax.broadcasted_iota(jnp.int32, (size, stack), 0)
            s = jnp.where((u >= begin_all) & (u <= token_all), s, -1e30)
            score[j] = s
            dprob[j] = lax.dot_general(v_all[kb], dout[...], NT, preferred_element_type=F32)
            return jnp.maximum(top, jnp.max(s, axis=0, keepdims=True))

        top = lax.fori_loop(0, count, scores, jnp.full((1, stack), -1e30, F32))

        def sums(j, carry):
            total, weighted = carry
            e = jnp.exp2((score[j] - top) * (scale * math.log2(math.e)))
            score[j] = e
            return (
                total + jnp.sum(e, axis=0, keepdims=True),
                weighted + jnp.sum(e * dprob[j], axis=0, keepdims=True),
            )

        zero = jnp.zeros((1, stack), F32)
        total, weighted = lax.fori_loop(0, count, sums, (zero, zero))
        share = 1.0 / total
        delta = weighted * share
        share_scaled = share * scale
        dqt[...] = jnp.zeros_like(dqt)

        def grads(j, carry):
            kb = first + j
            e = score[j]
            prob = (e * share).astype(BF16)
            ds = (e * share_scaled * (dprob[j] - delta)).astype(BF16)
            dqt[...] += lax.dot_general(kt_all[kb], ds, NN, preferred_element_type=F32)
            for h in range(group):
                at = slice(h * layers * size, (h + 1) * layers * size)
                acc[h, 0, kb] += lax.dot_general(
                    ds[:, at], normed[at, :], NN, preferred_element_type=F32
                )
                acc[h, 1, kb] += lax.dot_general(
                    prob[:, at], dout[at, :], NN, preferred_element_type=F32
                )
            return carry

        lax.fori_loop(0, count, grads, 0)

        for h in range(group):
            for layer in range(layers):
                at = slice((h * layers + layer) * size, (h * layers + layer + 1) * size)
                dnorm = dqt[:, at].T
                qhat, inv = norm_of(i, layer, h)
                dgain_ref[layer : layer + 1, :] += jnp.sum(dnorm * qhat, axis=0, keepdims=True)
                g = dnorm * gain_ref[layer : layer + 1, :]
                dq = inv * (g - qhat * jnp.mean(g * qhat, axis=-1, keepdims=True))
                dq = dq.astype(BF16)
                cols = slice(h * HD, (h + 1) * HD)
                for j in range(2):
                    dq_ref[2 * i + j, layer, :, cols] = dq[j * rows : (j + 1) * rows]
        return carry

    lax.fori_loop(0, half, q_block, 0)

    for b in range(half):
        for j in range(2):
            part = slice(j * rows, (j + 1) * rows)
            for kv in range(2):
                out = slice(kv * rows, (kv + 1) * rows)
                whole_sum = acc[0, kv, b, part, :]
                own = acc[0, kv, half + b, part, :]
                rounded = own.astype(BF16).astype(F32)
                for h in range(1, group):
                    whole_sum = whole_sum + acc[h, kv, b, part, :]
                    own = own + acc[h, kv, half + b, part, :]
                    rounded = rounded + acc[h, kv, half + b, part, :].astype(BF16).astype(F32)
                cross_ref[2 * b + j, out, :] = whole_sum.astype(BF16)
                own_ref[2 * b + j, out, :] = jnp.where(upper, rounded, own)


def total_over_devices(x):
    cores, ys = 2, 4
    half = cores * ys
    n_sp, n_dp = lax.axis_size("sp"), lax.axis_size("dp")
    xs = 4

    def pair(x, axis, perm):
        return x + lax.ppermute(x, axis, perm)

    def ring4(x, axis, shift):
        one, two, three = (lax.ppermute(x, axis, shift(k)) for k in (1, 2, 3))
        return (x + two) + (one + three)

    x = pair(x, "sp", [(s, s ^ 1) for s in range(n_sp)])
    x = ring4(
        x,
        "sp",
        lambda k: [
            (s, s // half * half + (s % half + k * cores) % half) for s in range(n_sp)
        ],
    )
    x = ring4(x, "dp", lambda k: [(d, d // xs * xs + (d + k) % xs) for d in range(n_dp)])
    x = ring4(x, "dp", lambda k: [(d, (d + k * xs) % n_dp) for d in range(n_dp)])
    return pair(x, "sp", [(s, (s + half) % n_sp) for s in range(n_sp)])


def on_device(queries, dout, keys, values, gain, segments):
    layers, _, rows, channels = queries.shape
    n_sp = lax.axis_size("sp")
    parts = n_sp // 2
    groups = [list(range(parts)), list(range(parts, n_sp))]
    low_to_up = [(s, s + parts) for s in range(parts)]
    up_to_low = [(s + parts, s) for s in range(parts)]
    width = channels // parts
    kv_width = keys.shape[2] // parts
    half = parts // 2
    size = 2 * rows
    stack = layers * (width // HD) * size
    upper = (lax.axis_index("sp") >= parts).astype(jnp.int32).reshape(1)

    def exchange(x):
        return lax.all_to_all(x, "sp", 0, 0, axis_index_groups=groups, tiled=True)

    kv_send = pl.pallas_call(
        pack_kv_kernel,
        out_shape=jax.ShapeDtypeStruct((parts, 2 * rows + IDS, kv_width), BF16),
        in_specs=[whole()] * 3,
        out_specs=whole(),
        compiler_params=params(16),
        name="pack_kv",
    )(keys[0], values[0], segments)
    kv_own = exchange(kv_send)
    qd_send = pl.pallas_call(
        pack_q_kernel,
        out_shape=jax.ShapeDtypeStruct((parts, 2 * layers, rows, width), BF16),
        in_specs=[whole()] * 2,
        out_specs=whole(),
        compiler_params=params(16),
        name="pack_q",
    )(queries[:, 0], dout[:, 0])
    qd = exchange(qd_send)
    kv_low = lax.ppermute(kv_own, "sp", low_to_up)

    dq_send, kv_sum, cross, dgain = pl.pallas_call(
        attention_kernel,
        out_shape=(
            jax.ShapeDtypeStruct((parts, layers, rows, width), BF16),
            jax.ShapeDtypeStruct((parts, 2 * rows, kv_width), F32),
            jax.ShapeDtypeStruct((parts, 2 * rows, kv_width), BF16),
            jax.ShapeDtypeStruct((8, HD), F32),
        ),
        in_specs=[pl.BlockSpec(memory_space=pltpu.SMEM)] + [whole()] * 4,
        out_specs=(whole(),) * 4,
        scratch_shapes=[
            pltpu.VMEM((2 * half, size, HD), BF16),
            pltpu.VMEM((2 * half, size, HD), BF16),
            pltpu.VMEM((2 * half, HD, size), BF16),
            pltpu.VMEM((half, 1, size), F32),
            pltpu.VMEM((stack, HD), BF16),
            pltpu.VMEM((stack, HD), BF16),
            pltpu.VMEM((half + 1, size, stack), F32),
            pltpu.VMEM((half + 1, size, stack), F32),
            pltpu.VMEM((width // HD, 2, 2 * half, size, HD), F32),
            pltpu.VMEM((HD, stack), F32),
        ],
        compiler_params=params(48),
        name="attention",
    )(upper, kv_own, kv_low, qd, gain)

    cross_low = lax.ppermute(cross, "sp", up_to_low)
    dq_recv = exchange(dq_send)
    kv_out = pl.pallas_call(
        combine_kernel,
        out_shape=jax.ShapeDtypeStruct((parts, 2 * rows, kv_width), BF16),
        in_specs=[whole()] * 2,
        out_specs=whole(),
        compiler_params=params(16),
        name="combine",
    )(kv_sum, cross_low)
    dkv_recv = exchange(kv_out)
    dgain = total_over_devices(dgain)[:layers]
    dqueries = pl.pallas_call(
        unpack_q_kernel,
        out_shape=jax.ShapeDtypeStruct((layers, rows, channels), BF16),
        in_specs=[whole()],
        out_specs=whole(),
        compiler_params=params(16),
        name="unpack_q",
    )(dq_recv)
    dkeys, dvalues = pl.pallas_call(
        unpack_kv_kernel,
        out_shape=(jax.ShapeDtypeStruct((rows, keys.shape[2]), BF16),) * 2,
        in_specs=[whole()],
        out_specs=(whole(),) * 2,
        compiler_params=params(16),
        name="unpack_kv",
    )(dkv_recv)
    return dqueries[:, None], dkeys[None], dvalues[None], dgain


def solution(mesh):
    return jax.shard_map(
        on_device,
        mesh=mesh,
        in_specs=(
            P(None, "dp", "sp", None),
            P(None, "dp", "sp", None),
            P("dp", "sp", None),
            P("dp", "sp", None),
            P(),
            P("dp", "sp"),
        ),
        out_specs=(P(None, "dp", "sp", None), P("dp", "sp", None), P("dp", "sp", None), P()),
        check_vma=False,
    )
```

```python
import functools
import math

import jax
import jax.numpy as jnp
from jax import lax
from jax.experimental import pallas as pl
from jax.experimental.pallas import tpu as pltpu
from jax.sharding import PartitionSpec as P

F32 = jnp.float32
BF16 = jnp.bfloat16
HD = 128
IDS = 16
PIECES = 3
GAIN_ROWS = 8
NT = (((1,), (1,)), ((), ()))
NN = (((1,), (0,)), ((), ()))


def params(mib):
    return pltpu.CompilerParams(vmem_limit_bytes=mib << 20)


def in_hbm():
    return pl.BlockSpec(memory_space=pltpu.HBM)


def whole():
    return pl.BlockSpec(memory_space=pltpu.VMEM)


def pack_kv_kernel(key_ref, value_ref, seg_ref, out_ref):
    parts, _, width = out_ref.shape
    rows = key_ref.shape[0]
    ids = jnp.broadcast_to(seg_ref[...].astype(F32), (IDS, rows)).astype(BF16)
    for h in range(parts):
        cols = slice(h * width, (h + 1) * width)
        out_ref[h, :rows, :] = key_ref[:, cols]
        out_ref[h, rows : 2 * rows, :] = value_ref[:, cols]
        out_ref[h, 2 * rows :, :] = ids


def pack_q_kernel(query_ref, dout_ref, out_ref):
    parts, twice, _, width = out_ref.shape
    layers = twice // 2
    for h in range(parts):
        cols = slice(h * width, (h + 1) * width)
        for layer in range(layers):
            out_ref[h, layer] = query_ref[layer, :, cols]
            out_ref[h, layers + layer] = dout_ref[layer, :, cols]


def unpack_q_kernel(in_ref, out_ref):
    parts, layers, _, width = in_ref.shape
    for h in range(parts):
        for layer in range(layers):
            out_ref[layer, :, h * width : (h + 1) * width] = in_ref[h, layer]


def combine_kernel(own_ref, cross_ref, dgain_ref, out_ref):
    twice = own_ref.shape[1]
    out_ref[:, :twice, :] = (own_ref[...] + cross_ref[...].astype(F32)).astype(BF16)
    rest = dgain_ref[...]
    pieces = []
    for _ in range(PIECES):
        piece = rest.astype(BF16).astype(F32)
        rest = rest - piece
        pieces.append(piece)
    pieces = jnp.concatenate(pieces + [jnp.zeros_like(rest)], 0).astype(BF16)
    for h in range(out_ref.shape[0]):
        out_ref[h, twice:, :] = pieces


def unpack_kv_kernel(in_ref, dk_ref, dv_ref, dgain_ref):
    parts, _, width = in_ref.shape
    rows = dk_ref.shape[0]
    total = jnp.zeros((GAIN_ROWS, width), F32)
    for h in range(parts):
        cols = slice(h * width, (h + 1) * width)
        dk_ref[:, cols] = in_ref[h, :rows, :]
        dv_ref[:, cols] = in_ref[h, rows : 2 * rows, :]
        pieces = in_ref[h, 2 * rows :, :].astype(F32)
        for n in range(PIECES):
            total = total + pieces[n * GAIN_ROWS : (n + 1) * GAIN_ROWS]
    dgain_ref[...] = total[: dgain_ref.shape[0]]


def attention_kernel(
    upper_ref,
    own_kv_ref,
    low_kv_ref,
    qd_ref,
    gain_ref,
    dq_ref,
    own_ref,
    cross_ref,
    dgain_ref,
    k_all,
    v_all,
    kt_all,
    start_all,
    qhat_t,
    inv_row,
    normed_t,
    dout,
    expo,
    dprob,
    tops,
    acc,
    dq_t,
    gain_acc,
    dq_out,
    own_out,
    cross_out,
    sem,
):
    blocks, layers, rows, width = dq_ref.shape
    group = width // HD
    size = 2 * rows
    half = blocks // 2
    scale = 1.0 / math.sqrt(HD)
    rate = scale * math.log2(math.e)
    upper = upper_ref[0] > 0
    chunks = [
        (slice((h * layers + layer) * size, (h * layers + layer + 1) * size), h, layer)
        for h in range(group)
        for layer in range(layers)
    ]

    def eye(n):
        at = lax.broadcasted_iota(jnp.int32, (n, n), 0)
        return (at == lax.broadcasted_iota(jnp.int32, (n, n), 1)).astype(F32)

    def dot(a, b, dims):
        return lax.dot_general(a, b, dims, preferred_element_type=F32)

    unit = eye(HD).astype(BF16)
    unit_size = eye(size).astype(BF16)
    gain_cols = [
        jnp.sum(eye(HD) * gain_ref[layer : layer + 1, :], axis=1, keepdims=True)
        for layer in range(layers)
    ]

    for side, ref in enumerate((low_kv_ref, own_kv_ref)):
        for b in range(half):
            at = side * half + b
            for j in range(2):
                part = slice(j * rows, (j + 1) * rows)
                k_all[at, part, :] = ref[2 * b + j, :rows, :]
                v_all[at, part, :] = ref[2 * b + j, rows : 2 * rows, :]
            kt_all[at] = dot(unit, k_all[at], NT).astype(BF16)

    ids_own = jnp.concatenate(
        [own_kv_ref[b, 2 * rows :, :][:1].astype(F32) for b in range(blocks)], 0
    )
    ids_low = jnp.concatenate(
        [low_kv_ref[b, 2 * rows :, :][:1].astype(F32) for b in range(blocks)], 0
    )
    begin = jnp.zeros((blocks, rows), F32)
    for doc in range(8):
        below = jnp.sum((ids_own < doc).astype(F32), keepdims=True)
        below_low = jnp.sum((ids_low < doc).astype(F32), keepdims=True)
        total = below + jnp.where(upper, below_low, float(blocks * rows))
        begin = jnp.where(ids_own == doc, total, begin)
    for b in range(half):
        start_all[b] = jnp.concatenate([begin[2 * b : 2 * b + 1], begin[2 * b + 1 : 2 * b + 2]], 1)

    acc[...] = jnp.zeros_like(acc)
    gain_acc[...] = jnp.zeros_like(gain_acc)

    def part_of(i, layer, h, offset):
        cols = slice(h * HD, (h + 1) * HD)
        return jnp.concatenate(
            [qd_ref[2 * i + j, offset + layer, :, cols] for j in range(2)], 0
        )

    def q_block(i, carry):
        for at, h, layer in chunks:
            q = dot(unit, part_of(i, layer, h, 0), NT)
            inv = lax.rsqrt(jnp.mean(q * q, axis=0, keepdims=True) + 1e-6)
            qhat = q * inv
            inv_row[:, at] = inv
            qhat_t[:, at] = qhat
            normed_t[:, at] = (qhat * gain_cols[layer]).astype(BF16)
            dout[at, :] = part_of(i, layer, h, layers)
        begin_row = start_all[i]
        first = jnp.min(begin_row).astype(jnp.int32) // size
        last = half + i
        count = last - first + 1
        begin_int = begin_row.astype(jnp.int32)
        token = last * size + lax.broadcasted_iota(jnp.int32, (1, size), 1)
        dq_t[...] = jnp.zeros_like(dq_t)

        def sums(j, carry):
            kb = first + j
            k, v = k_all[kb], v_all[kb]
            u = kb * size + lax.broadcasted_iota(jnp.int32, (size, size), 0)
            bias = jnp.where((u >= begin_int) & (u <= token), 0.0, -1e30)
            out = []
            for (at, _, _), (top, total, weighted) in zip(chunks, carry):
                s = dot(k, normed_t[:, at], NN) + bias
                dp = dot(v, dout[at, :], NT)
                new = jnp.maximum(top, jnp.max(s, axis=0, keepdims=True))
                e = jnp.exp2((s - new) * rate)
                keep = jnp.exp2((top - new) * rate)
                expo[j, :, at] = e
                dprob[j, :, at] = dp
                tops[j, :, at] = new
                out.append(
                    (
                        new,
                        total * keep + jnp.sum(e, axis=0, keepdims=True),
                        weighted * keep + jnp.sum(e * dp, axis=0, keepdims=True),
                    )
                )
            return tuple(out)

        zero = jnp.zeros((1, size), F32)
        low = jnp.full((1, size), -1e30, F32)
        stats = lax.fori_loop(0, count, sums, ((low, zero, zero),) * len(chunks))
        shares = [1.0 / total for _, total, _ in stats]
        deltas = [weighted * share for (_, _, weighted), share in zip(stats, shares)]

        def grads(j, carry):
            kb = first + j
            kt = kt_all[kb]
            probs, scores = [], []
            for (at, _, _), (top, _, _), share, delta in zip(chunks, stats, shares, deltas):
                prob = expo[j, :, at] * (share * jnp.exp2((tops[j, :, at] - top) * rate))
                ds = (prob * ((dprob[j, :, at] - delta) * scale)).astype(BF16)
                probs.append(prob.astype(BF16))
                scores.append(ds)
                dq_t[:, at] += dot(kt, ds, NN)
            for h in range(group):
                at = slice(h * layers * size, (h + 1) * layers * size)
                mine = slice(h * layers, (h + 1) * layers)
                ds = jnp.concatenate(scores[mine], 1)
                prob = jnp.concatenate(probs[mine], 1)
                acc[h, 0, kb] += dot(ds, normed_t[:, at], NT)
                acc[h, 1, kb] += dot(prob, dout[at, :], NN)
            return carry

        lax.fori_loop(0, count, grads, 0)

        for at, h, layer in chunks:
            dnorm, qhat = dq_t[:, at], qhat_t[:, at]
            part = dnorm * qhat
            gain_acc[layer] += part[:, :rows] + part[:, rows:]
            g = dnorm * gain_cols[layer]
            dq = inv_row[:, at] * (g - qhat * jnp.mean(g * qhat, axis=0, keepdims=True))
            dq = dot(unit_size, dq.astype(BF16), NT).astype(BF16)
            cols = slice(h * HD, (h + 1) * HD)
            for j in range(2):
                dq_out[2 * i + j, layer, :, cols] = dq[j * rows : (j + 1) * rows]
        pair = pl.ds(2 * i, 2)
        pltpu.make_async_copy(dq_out.at[pair], dq_ref.at[pair], sem.at[i]).start()
        return carry

    lax.fori_loop(0, half, q_block, 0)

    dgain_ref[...] = jnp.zeros_like(dgain_ref)
    for layer in range(layers):
        dgain_ref[layer : layer + 1, :] = jnp.sum(gain_acc[layer].T, axis=0, keepdims=True)
    copies = []
    for b in range(half):
        for j in range(2):
            part = slice(j * rows, (j + 1) * rows)
            for kv in range(2):
                out = slice(kv * rows, (kv + 1) * rows)
                whole_sum = acc[0, kv, b, part, :]
                own = acc[0, kv, half + b, part, :]
                rounded = own.astype(BF16).astype(F32)
                for h in range(1, group):
                    whole_sum = whole_sum + acc[h, kv, b, part, :]
                    own = own + acc[h, kv, half + b, part, :]
                    rounded = rounded + acc[h, kv, half + b, part, :].astype(BF16).astype(F32)
                cross_out[2 * b + j, out, :] = whole_sum.astype(BF16)
                own_out[2 * b + j, out, :] = jnp.where(upper, rounded, own)
        pair = pl.ds(2 * b, 2)
        for n, (src, dst) in enumerate(((cross_out, cross_ref), (own_out, own_ref))):
            copy = pltpu.make_async_copy(src.at[pair], dst.at[pair], sem.at[half * (n + 1) + b])
            copy.start()
            copies.append(copy)
    for b in range(half):
        pair = pl.ds(2 * b, 2)
        pltpu.make_async_copy(dq_out.at[pair], dq_ref.at[pair], sem.at[b]).wait()
    for copy in copies:
        copy.wait()


def attention(upper, kv_own, kv_low, qd, gain):
    parts, twice, rows, width = qd.shape
    layers = twice // 2
    kv_width = kv_own.shape[2]
    half = parts // 2
    size = 2 * rows
    stack = layers * (width // HD) * size
    return pl.pallas_call(
        attention_kernel,
        out_shape=(
            jax.ShapeDtypeStruct((parts, layers, rows, width), BF16),
            jax.ShapeDtypeStruct((parts, 2 * rows, kv_width), F32),
            jax.ShapeDtypeStruct((parts, 2 * rows, kv_width), BF16),
            jax.ShapeDtypeStruct((8, HD), F32),
        ),
        in_specs=[pl.BlockSpec(memory_space=pltpu.SMEM)] + [whole()] * 4,
        out_specs=(in_hbm(),) * 3 + (whole(),),
        scratch_shapes=[
            pltpu.VMEM((2 * half, size, HD), BF16),
            pltpu.VMEM((2 * half, size, HD), BF16),
            pltpu.VMEM((2 * half, HD, size), BF16),
            pltpu.VMEM((half, 1, size), F32),
            pltpu.VMEM((HD, stack), F32),
            pltpu.VMEM((1, stack), F32),
            pltpu.VMEM((HD, stack), BF16),
            pltpu.VMEM((stack, HD), BF16),
            pltpu.VMEM((half + 1, size, stack), F32),
            pltpu.VMEM((half + 1, size, stack), F32),
            pltpu.VMEM((half + 1, 1, stack), F32),
            pltpu.VMEM((width // HD, 2, 2 * half, size, HD), F32),
            pltpu.VMEM((HD, stack), F32),
            pltpu.VMEM((layers, HD, rows), F32),
            pltpu.VMEM((parts, layers, rows, width), BF16),
            pltpu.VMEM((parts, 2 * rows, kv_width), F32),
            pltpu.VMEM((parts, 2 * rows, kv_width), BF16),
            pltpu.SemaphoreType.DMA((3 * half,)),
        ],
        compiler_params=params(52),
        name="attention",
    )(upper, kv_own, kv_low, qd, gain)


RING = 4


def pair_sum(x, axis, perm):
    return x + lax.ppermute(x, axis, perm)


def ring_sum(x, axis, shift):
    one, two, three = (lax.ppermute(x, axis, shift(k)) for k in (1, 2, 3))
    return (x + two) + (one + three)


def over_x(x):
    return ring_sum(
        x,
        "dp",
        lambda k: [
            (d, d // RING * RING + (d + k) % RING) for d in range(lax.axis_size("dp"))
        ],
    )


def over_z(x):
    n_sp, n_dp = lax.axis_size("sp"), lax.axis_size("dp")
    x = ring_sum(x, "dp", lambda k: [(d, (d + k * RING) % n_dp) for d in range(n_dp)])
    return pair_sum(x, "sp", [(s, (s + n_sp // 2) % n_sp) for s in range(n_sp)])


def on_device(queries, dout, keys, values, gain, segments):
    layers, _, rows, channels = queries.shape
    n_sp = lax.axis_size("sp")
    parts = n_sp // 2
    groups = [list(range(parts)), list(range(parts, n_sp))]
    low_to_up = [(s, s + parts) for s in range(parts)]
    up_to_low = [(s + parts, s) for s in range(parts)]
    width = channels // parts
    kv_width = keys.shape[2] // parts
    upper = (lax.axis_index("sp") >= parts).astype(jnp.int32).reshape(1)

    def exchange(x):
        return lax.all_to_all(x, "sp", 0, 0, axis_index_groups=groups, tiled=True)

    kv_send = pl.pallas_call(
        pack_kv_kernel,
        out_shape=jax.ShapeDtypeStruct((parts, 2 * rows + IDS, kv_width), BF16),
        in_specs=[whole()] * 3,
        out_specs=whole(),
        compiler_params=params(63),
        name="pack_kv",
    )(keys[0], values[0], segments)
    kv_own = exchange(kv_send)
    queries, dout, _ = lax.optimization_barrier((queries, dout, kv_send))
    qd_send = pl.pallas_call(
        pack_q_kernel,
        out_shape=jax.ShapeDtypeStruct((parts, 2 * layers, rows, width), BF16),
        in_specs=[whole()] * 2,
        out_specs=whole(),
        compiler_params=params(63),
        name="pack_q",
    )(queries[:, 0], dout[:, 0])
    kv_low = lax.ppermute(kv_own, "sp", low_to_up)
    qd = exchange(qd_send)

    dq_send, kv_sum, cross, dgain = attention(upper, kv_own, kv_low, qd, gain)

    cross_low = lax.ppermute(cross, "sp", up_to_low)
    dgain = over_x(dgain)
    dq_recv = exchange(dq_send)
    dgain = over_z(dgain)
    kv_out = pl.pallas_call(
        combine_kernel,
        out_shape=jax.ShapeDtypeStruct(
            (parts, 2 * rows + (PIECES + 1) * GAIN_ROWS, kv_width), BF16
        ),
        in_specs=[whole()] * 3,
        out_specs=whole(),
        compiler_params=params(16),
        name="combine",
    )(kv_sum, cross_low, dgain)
    dkv_recv = exchange(kv_out)
    dqueries = pl.pallas_call(
        unpack_q_kernel,
        out_shape=jax.ShapeDtypeStruct((layers, rows, channels), BF16),
        in_specs=[whole()],
        out_specs=whole(),
        compiler_params=params(16),
        name="unpack_q",
    )(dq_recv)
    dkeys, dvalues, dgain = pl.pallas_call(
        unpack_kv_kernel,
        out_shape=(jax.ShapeDtypeStruct((rows, keys.shape[2]), BF16),) * 2
        + (jax.ShapeDtypeStruct(gain.shape, F32),),
        in_specs=[whole()],
        out_specs=(whole(),) * 3,
        compiler_params=params(16),
        name="unpack_kv",
    )(dkv_recv)
    return dqueries[:, None], dkeys[None], dvalues[None], dgain


def solution(mesh):
    return jax.shard_map(
        on_device,
        mesh=mesh,
        in_specs=(
            P(None, "dp", "sp", None),
            P(None, "dp", "sp", None),
            P("dp", "sp", None),
            P("dp", "sp", None),
            P(),
            P("dp", "sp"),
        ),
        out_specs=(P(None, "dp", "sp", None), P("dp", "sp", None), P("dp", "sp", None), P()),
        check_vma=False,
    )
```

```python
import functools
import math

import jax
import jax.numpy as jnp
from jax import lax
from jax.experimental import pallas as pl
from jax.experimental.pallas import tpu as pltpu
from jax.sharding import PartitionSpec as P

F32 = jnp.float32
BF16 = jnp.bfloat16
HD = 128
IDS = 16
PIECES = 3
GAIN_ROWS = 8
NT = (((1,), (1,)), ((), ()))
NN = (((1,), (0,)), ((), ()))


def params(mib):
    return pltpu.CompilerParams(vmem_limit_bytes=mib << 20)


def in_hbm():
    return pl.BlockSpec(memory_space=pltpu.HBM)


def whole():
    return pl.BlockSpec(memory_space=pltpu.VMEM)


def pack_kv_kernel(key_ref, value_ref, seg_ref, out_ref):
    parts, _, width = out_ref.shape
    rows = key_ref.shape[0]
    ids = jnp.broadcast_to(seg_ref[...].astype(F32), (IDS, rows)).astype(BF16)
    for h in range(parts):
        cols = slice(h * width, (h + 1) * width)
        out_ref[h, :rows, :] = key_ref[:, cols]
        out_ref[h, rows : 2 * rows, :] = value_ref[:, cols]
        out_ref[h, 2 * rows :, :] = ids


def pack_q_kernel(query_ref, dout_ref, out_ref):
    parts, twice, _, width = out_ref.shape
    layers = twice // 2
    for h in range(parts):
        cols = slice(h * width, (h + 1) * width)
        for layer in range(layers):
            out_ref[h, layer] = query_ref[layer, :, cols]
            out_ref[h, layers + layer] = dout_ref[layer, :, cols]


def unpack_q_kernel(in_ref, out_ref):
    parts, layers, _, width = in_ref.shape
    for h in range(parts):
        for layer in range(layers):
            out_ref[layer, :, h * width : (h + 1) * width] = in_ref[h, layer]


def combine_kernel(own_ref, cross_ref, dgain_ref, out_ref):
    twice = own_ref.shape[1]
    out_ref[:, :twice, :] = (own_ref[...] + cross_ref[...].astype(F32)).astype(BF16)
    rest = dgain_ref[...]
    pieces = []
    for _ in range(PIECES):
        piece = rest.astype(BF16).astype(F32)
        rest = rest - piece
        pieces.append(piece)
    pieces = jnp.concatenate(pieces + [jnp.zeros_like(rest)], 0).astype(BF16)
    for h in range(out_ref.shape[0]):
        out_ref[h, twice:, :] = pieces


def unpack_kv_kernel(in_ref, dk_ref, dv_ref, dgain_ref):
    parts, _, width = in_ref.shape
    rows = dk_ref.shape[0]
    total = jnp.zeros((GAIN_ROWS, width), F32)
    for h in range(parts):
        cols = slice(h * width, (h + 1) * width)
        dk_ref[:, cols] = in_ref[h, :rows, :]
        dv_ref[:, cols] = in_ref[h, rows : 2 * rows, :]
        pieces = in_ref[h, 2 * rows :, :].astype(F32)
        for n in range(PIECES):
            total = total + pieces[n * GAIN_ROWS : (n + 1) * GAIN_ROWS]
    dgain_ref[...] = total[: dgain_ref.shape[0]]


def attention_kernel(
    upper_ref,
    own_kv_ref,
    low_kv_ref,
    qd_hbm,
    gain_ref,
    dq_ref,
    own_ref,
    cross_ref,
    dgain_ref,
    k_all,
    v_all,
    kt_all,
    start_all,
    qhat_t,
    inv_row,
    normed_t,
    dout,
    expo,
    dprob,
    tops,
    acc_k,
    acc_v,
    dq_t,
    gain_acc,
    first_all,
    qd_ref,
    qd_sem,
    dq_out,
    own_out,
    cross_out,
    sem,
):
    blocks, layers, rows, width = dq_ref.shape
    group = width // HD
    size = 2 * rows
    half = blocks // 2
    scale = 1.0 / math.sqrt(HD)
    rate = scale * math.log2(math.e)
    upper = upper_ref[0] > 0
    chunks = [
        (slice((h * layers + layer) * size, (h * layers + layer + 1) * size), h, layer)
        for h in range(group)
        for layer in range(layers)
    ]

    def eye(n):
        at = lax.broadcasted_iota(jnp.int32, (n, n), 0)
        return (at == lax.broadcasted_iota(jnp.int32, (n, n), 1)).astype(F32)

    def dot(a, b, dims):
        return lax.dot_general(a, b, dims, preferred_element_type=F32)

    def load(i):
        pair = pl.ds(2 * i, 2)
        return pltpu.make_async_copy(qd_hbm.at[pair], qd_ref.at[pair], qd_sem.at[i])

    for i in range(half):
        load(i).start()

    unit = eye(HD).astype(BF16)
    gain_cols = [
        jnp.sum(eye(HD) * gain_ref[layer : layer + 1, :], axis=1, keepdims=True)
        for layer in range(layers)
    ]

    for side, ref in enumerate((low_kv_ref, own_kv_ref)):
        for b in range(half):
            at = side * half + b
            for j in range(2):
                part = slice(j * rows, (j + 1) * rows)
                k_all[at, part, :] = ref[2 * b + j, :rows, :]
                v_all[at, part, :] = ref[2 * b + j, rows : 2 * rows, :]
            kt_all[at] = dot(unit, k_all[at], NT).astype(BF16)

    ids_own = jnp.concatenate(
        [own_kv_ref[b, 2 * rows :, :][:1].astype(F32) for b in range(blocks)], 0
    )
    ids_low = jnp.concatenate(
        [low_kv_ref[b, 2 * rows :, :][:1].astype(F32) for b in range(blocks)], 0
    )
    begin = jnp.zeros((blocks, rows), F32)
    for doc in range(8):
        below = jnp.sum((ids_own < doc).astype(F32), keepdims=True)
        below_low = jnp.sum((ids_low < doc).astype(F32), keepdims=True)
        total = below + jnp.where(upper, below_low, float(blocks * rows))
        begin = jnp.where(ids_own == doc, total, begin)
    for b in range(half):
        start_all[b] = jnp.concatenate([begin[2 * b : 2 * b + 1], begin[2 * b + 1 : 2 * b + 2]], 1)
        first_all[b] = jnp.min(begin[2 * b : 2 * b + 1]).astype(jnp.int32) // size

    acc_k[...] = jnp.zeros_like(acc_k)
    acc_v[...] = jnp.zeros_like(acc_v)
    gain_acc[...] = jnp.zeros_like(gain_acc)

    def part_of(i, layer, h, offset):
        cols = slice(h * HD, (h + 1) * HD)
        return jnp.concatenate(
            [qd_ref[2 * i + j, offset + layer, :, cols] for j in range(2)], 0
        )

    def q_block(i, carry):
        load(i).wait()
        q_all = jnp.concatenate([part_of(i, layer, h, 0) for _, h, layer in chunks], 0)
        q_all = dot(unit, q_all, NT)
        for at, h, layer in chunks:
            q = q_all[:, at]
            inv = lax.rsqrt(jnp.mean(q * q, axis=0, keepdims=True) + 1e-6)
            qhat = q * inv
            inv_row[:, at] = inv
            qhat_t[:, at] = qhat
            normed_t[:, at] = (qhat * gain_cols[layer]).astype(BF16)
            dout[at, :] = part_of(i, layer, h, layers)
        begin_row = start_all[i]
        first = first_all[i]
        last = half + i
        count = last - first + 1
        begin_int = begin_row.astype(jnp.int32)
        token = last * size + lax.broadcasted_iota(jnp.int32, (1, size), 1)
        dq_t[...] = jnp.zeros_like(dq_t)

        def sums(j, n, carry):
            kb = first + j
            k, v = k_all[kb], v_all[kb]
            u = kb * size + lax.broadcasted_iota(jnp.int32, (size, size), 0)
            allowed = u >= begin_int
            if j == n - 1:
                allowed = allowed & (u <= token)
            bias = jnp.where(allowed, 0.0, -1e30)
            out = []
            for (at, _, _), (top, total, weighted) in zip(chunks, carry):
                s = dot(k, normed_t[:, at], NN) + bias
                dp = dot(v, dout[at, :], NT)
                new = jnp.maximum(top, jnp.max(s, axis=0, keepdims=True))
                e = jnp.exp2((s - new) * rate)
                keep = jnp.exp2((top - new) * rate)
                expo[j, :, at] = e
                dprob[j, :, at] = dp
                tops[j, :, at] = new
                out.append(
                    (
                        new,
                        total * keep + jnp.sum(e, axis=0, keepdims=True),
                        weighted * keep + jnp.sum(e * dp, axis=0, keepdims=True),
                    )
                )
            return tuple(out)

        zero = jnp.zeros((1, size), F32)
        low = jnp.full((1, size), -1e30, F32)
        def run(n):
            stats = ((low, zero, zero),) * len(chunks)
            for j in range(n):
                stats = sums(j, n, stats)
            shares = [1.0 / total for _, total, _ in stats]
            deltas = [weighted * share for (_, _, weighted), share in zip(stats, shares)]

            def grads(j, carry):
                kb = first + j
                kt = kt_all[kb]
                probs, scores = [], []
                for (at, _, _), (top, _, _), share, delta in zip(chunks, stats, shares, deltas):
                    prob = expo[j, :, at] * (share * jnp.exp2((tops[j, :, at] - top) * rate))
                    ds = (prob * ((dprob[j, :, at] - delta) * scale)).astype(BF16)
                    probs.append(prob.astype(BF16))
                    scores.append(ds)
                    dq_t[:, at] += dot(kt, ds, NN)
                acc_k[kb] += dot(jnp.concatenate(scores, 1), normed_t[...], NT)
                acc_v[kb] += dot(jnp.concatenate(probs, 1), dout[...], NN)
                return carry

            for j in range(n):
                grads(j, 0)

        for n in range(1, half + 2):
            pl.when(count == n)(functools.partial(run, n))

        for at, h, layer in chunks:
            dnorm, qhat = dq_t[:, at], qhat_t[:, at]
            part = dnorm * qhat
            gain_acc[layer] += part[:, :rows] + part[:, rows:]
            g = dnorm * gain_cols[layer]
            dq = inv_row[:, at] * (g - qhat * jnp.mean(g * qhat, axis=0, keepdims=True))
            dq = dq.T.astype(BF16)
            cols = slice(h * HD, (h + 1) * HD)
            for j in range(2):
                dq_out[2 * i + j, layer, :, cols] = dq[j * rows : (j + 1) * rows]
        pair = pl.ds(2 * i, 2)
        pltpu.make_async_copy(dq_out.at[pair], dq_ref.at[pair], sem.at[i]).start()
        return carry

    lax.fori_loop(0, half, q_block, 0)

    dgain_ref[...] = jnp.zeros_like(dgain_ref)
    for layer in range(layers):
        dgain_ref[layer : layer + 1, :] = jnp.sum(gain_acc[layer].T, axis=0, keepdims=True)
    copies = []
    for b in range(half):
        for j in range(2):
            part = slice(j * rows, (j + 1) * rows)
            for kv, acc in enumerate((acc_k, acc_v)):
                out = slice(kv * rows, (kv + 1) * rows)
                cross_out[2 * b + j, out, :] = acc[b, part, :].astype(BF16)
                own_out[2 * b + j, out, :] = acc[half + b, part, :]
        pair = pl.ds(2 * b, 2)
        for n, (src, dst) in enumerate(((cross_out, cross_ref), (own_out, own_ref))):
            copy = pltpu.make_async_copy(src.at[pair], dst.at[pair], sem.at[half * (n + 1) + b])
            copy.start()
            copies.append(copy)
    for b in range(half):
        pair = pl.ds(2 * b, 2)
        pltpu.make_async_copy(dq_out.at[pair], dq_ref.at[pair], sem.at[b]).wait()
    for copy in copies:
        copy.wait()


def attention(upper, kv_own, kv_low, qd, gain):
    parts, twice, rows, width = qd.shape
    layers = twice // 2
    kv_width = kv_own.shape[2]
    half = parts // 2
    size = 2 * rows
    stack = layers * (width // HD) * size
    return pl.pallas_call(
        attention_kernel,
        out_shape=(
            jax.ShapeDtypeStruct((parts, layers, rows, width), BF16),
            jax.ShapeDtypeStruct((parts, 2 * rows, kv_width), F32),
            jax.ShapeDtypeStruct((parts, 2 * rows, kv_width), BF16),
            jax.ShapeDtypeStruct((8, HD), F32),
        ),
        in_specs=[pl.BlockSpec(memory_space=pltpu.SMEM), whole(), whole(), in_hbm(), whole()],
        out_specs=(in_hbm(),) * 3 + (whole(),),
        scratch_shapes=[
            pltpu.VMEM((2 * half, size, HD), BF16),
            pltpu.VMEM((2 * half, size, HD), BF16),
            pltpu.VMEM((2 * half, HD, size), BF16),
            pltpu.VMEM((half, 1, size), F32),
            pltpu.VMEM((HD, stack), F32),
            pltpu.VMEM((1, stack), F32),
            pltpu.VMEM((HD, stack), BF16),
            pltpu.VMEM((stack, HD), BF16),
            pltpu.VMEM((half + 1, size, stack), F32),
            pltpu.VMEM((half + 1, size, stack), F32),
            pltpu.VMEM((half + 1, 1, stack), F32),
            pltpu.VMEM((2 * half, size, HD), F32),
            pltpu.VMEM((2 * half, size, HD), F32),
            pltpu.VMEM((HD, stack), F32),
            pltpu.VMEM((layers, HD, rows), F32),
            pltpu.SMEM((half,), jnp.int32),
            pltpu.VMEM((parts, twice, rows, width), BF16),
            pltpu.SemaphoreType.DMA((half,)),
            pltpu.VMEM((parts, layers, rows, width), BF16),
            pltpu.VMEM((parts, 2 * rows, kv_width), F32),
            pltpu.VMEM((parts, 2 * rows, kv_width), BF16),
            pltpu.SemaphoreType.DMA((3 * half,)),
        ],
        compiler_params=params(52),
        name="attention",
    )(upper, kv_own, kv_low, qd, gain)


RING = 4


def pair_sum(x, axis, perm):
    return x + lax.ppermute(x, axis, perm)


def ring_sum(x, axis, shift):
    one, two, three = (lax.ppermute(x, axis, shift(k)) for k in (1, 2, 3))
    return (x + two) + (one + three)


def over_x(x):
    return ring_sum(
        x,
        "dp",
        lambda k: [
            (d, d // RING * RING + (d + k) % RING) for d in range(lax.axis_size("dp"))
        ],
    )


def over_z(x):
    n_sp, n_dp = lax.axis_size("sp"), lax.axis_size("dp")
    x = ring_sum(x, "dp", lambda k: [(d, (d + k * RING) % n_dp) for d in range(n_dp)])
    return pair_sum(x, "sp", [(s, (s + n_sp // 2) % n_sp) for s in range(n_sp)])


def on_device(queries, dout, keys, values, gain, segments):
    layers, _, rows, channels = queries.shape
    n_sp = lax.axis_size("sp")
    parts = n_sp // 2
    groups = [list(range(parts)), list(range(parts, n_sp))]
    low_to_up = [(s, s + parts) for s in range(parts)]
    up_to_low = [(s + parts, s) for s in range(parts)]
    width = channels // parts
    kv_width = keys.shape[2] // parts
    upper = (lax.axis_index("sp") >= parts).astype(jnp.int32).reshape(1)

    def exchange(x):
        return lax.all_to_all(x, "sp", 0, 0, axis_index_groups=groups, tiled=True)

    kv_send = pl.pallas_call(
        pack_kv_kernel,
        out_shape=jax.ShapeDtypeStruct((parts, 2 * rows + IDS, kv_width), BF16),
        in_specs=[whole()] * 3,
        out_specs=whole(),
        compiler_params=params(63),
        name="pack_kv",
    )(keys[0], values[0], segments)
    kv_own = exchange(kv_send)
    queries, dout, _ = lax.optimization_barrier((queries, dout, kv_send))
    qd_send = pl.pallas_call(
        pack_q_kernel,
        out_shape=jax.ShapeDtypeStruct((parts, 2 * layers, rows, width), BF16),
        in_specs=[whole()] * 2,
        out_specs=whole(),
        compiler_params=params(63),
        name="pack_q",
    )(queries[:, 0], dout[:, 0])
    kv_low = lax.ppermute(kv_own, "sp", low_to_up)
    qd = exchange(qd_send)

    dq_send, kv_sum, cross, dgain = attention(upper, kv_own, kv_low, qd, gain)

    cross_low = lax.ppermute(cross, "sp", up_to_low)
    dgain = over_x(dgain)
    dq_recv = exchange(dq_send)
    dgain = over_z(dgain)
    kv_out = pl.pallas_call(
        combine_kernel,
        out_shape=jax.ShapeDtypeStruct(
            (parts, 2 * rows + (PIECES + 1) * GAIN_ROWS, kv_width), BF16
        ),
        in_specs=[whole()] * 3,
        out_specs=whole(),
        compiler_params=params(16),
        name="combine",
    )(kv_sum, cross_low, dgain)
    dkv_recv = exchange(kv_out)
    dqueries = pl.pallas_call(
        unpack_q_kernel,
        out_shape=jax.ShapeDtypeStruct((layers, rows, channels), BF16),
        in_specs=[whole()],
        out_specs=whole(),
        compiler_params=params(16),
        name="unpack_q",
    )(dq_recv)
    dkeys, dvalues, dgain = pl.pallas_call(
        unpack_kv_kernel,
        out_shape=(jax.ShapeDtypeStruct((rows, keys.shape[2]), BF16),) * 2
        + (jax.ShapeDtypeStruct(gain.shape, F32),),
        in_specs=[whole()],
        out_specs=(whole(),) * 3,
        compiler_params=params(16),
        name="unpack_kv",
    )(dkv_recv)
    return dqueries[:, None], dkeys[None], dvalues[None], dgain


def solution(mesh):
    return jax.shard_map(
        on_device,
        mesh=mesh,
        in_specs=(
            P(None, "dp", "sp", None),
            P(None, "dp", "sp", None),
            P("dp", "sp", None),
            P("dp", "sp", None),
            P(),
            P("dp", "sp"),
        ),
        out_specs=(P(None, "dp", "sp", None), P("dp", "sp", None), P("dp", "sp", None), P()),
        check_vma=False,
    )
```

```python
import functools
import math

import jax
import jax.numpy as jnp
from jax import lax
from jax.experimental import pallas as pl
from jax.experimental.pallas import tpu as pltpu
from jax.sharding import PartitionSpec as P

F32 = jnp.float32
BF16 = jnp.bfloat16
HD = 128
IDS = 16
PIECES = 3
GAIN_ROWS = 8
NT = (((1,), (1,)), ((), ()))
NN = (((1,), (0,)), ((), ()))


def params(mib):
    return pltpu.CompilerParams(vmem_limit_bytes=mib << 20)


def in_hbm():
    return pl.BlockSpec(memory_space=pltpu.HBM)


def whole():
    return pl.BlockSpec(memory_space=pltpu.VMEM)


def pack_kv_kernel(key_ref, value_ref, seg_ref, out_ref):
    parts, _, width = out_ref.shape
    rows = key_ref.shape[0]
    ids = jnp.broadcast_to(seg_ref[...].astype(F32), (IDS, rows)).astype(BF16)
    for h in range(parts):
        cols = slice(h * width, (h + 1) * width)
        out_ref[h, :rows, :] = key_ref[:, cols]
        out_ref[h, rows : 2 * rows, :] = value_ref[:, cols]
        out_ref[h, 2 * rows :, :] = ids


def pack_q_kernel(query_ref, dout_ref, out_ref):
    parts, twice, _, width = out_ref.shape
    layers = twice // 2
    for h in range(parts):
        cols = slice(h * width, (h + 1) * width)
        for layer in range(layers):
            out_ref[h, layer] = query_ref[layer, :, cols]
            out_ref[h, layers + layer] = dout_ref[layer, :, cols]


def unpack_q_kernel(in_ref, out_ref):
    parts, layers, _, width = in_ref.shape
    for h in range(parts):
        for layer in range(layers):
            out_ref[layer, :, h * width : (h + 1) * width] = in_ref[h, layer]


def combine_kernel(own_ref, cross_ref, dgain_ref, out_ref):
    twice = own_ref.shape[1]
    out_ref[:, :twice, :] = (own_ref[...] + cross_ref[...].astype(F32)).astype(BF16)
    rest = dgain_ref[...]
    pieces = []
    for _ in range(PIECES):
        piece = rest.astype(BF16).astype(F32)
        rest = rest - piece
        pieces.append(piece)
    pieces = jnp.concatenate(pieces + [jnp.zeros_like(rest)], 0).astype(BF16)
    for h in range(out_ref.shape[0]):
        out_ref[h, twice:, :] = pieces


def unpack_kv_kernel(in_ref, dk_ref, dv_ref, dgain_ref):
    parts, _, width = in_ref.shape
    rows = dk_ref.shape[0]
    total = jnp.zeros((GAIN_ROWS, width), F32)
    for h in range(parts):
        cols = slice(h * width, (h + 1) * width)
        dk_ref[:, cols] = in_ref[h, :rows, :]
        dv_ref[:, cols] = in_ref[h, rows : 2 * rows, :]
        pieces = in_ref[h, 2 * rows :, :].astype(F32)
        for n in range(PIECES):
            total = total + pieces[n * GAIN_ROWS : (n + 1) * GAIN_ROWS]
    dgain_ref[...] = total[: dgain_ref.shape[0]]


def attention_kernel(
    upper_ref,
    own_kv_ref,
    low_kv_ref,
    qd_hbm,
    gain_ref,
    dq_ref,
    own_ref,
    cross_ref,
    dgain_ref,
    k_all,
    v_all,
    kt_all,
    start_all,
    qhat_t,
    inv_row,
    normed_t,
    dout,
    expo,
    dprob,
    tops,
    acc_k,
    acc_v,
    dq_t,
    gain_acc,
    first_all,
    dscore,
    qd_ref,
    qd_sem,
    dq_out,
    own_out,
    cross_out,
    sem,
):
    blocks, layers, rows, width = dq_ref.shape
    group = width // HD
    size = 2 * rows
    half = blocks // 2
    scale = 1.0 / math.sqrt(HD)
    rate = scale * math.log2(math.e)
    upper = upper_ref[0] > 0
    chunks = [
        (slice((h * layers + layer) * size, (h * layers + layer + 1) * size), h, layer)
        for h in range(group)
        for layer in range(layers)
    ]

    def eye(n):
        at = lax.broadcasted_iota(jnp.int32, (n, n), 0)
        return (at == lax.broadcasted_iota(jnp.int32, (n, n), 1)).astype(F32)

    def dot(a, b, dims):
        return lax.dot_general(a, b, dims, preferred_element_type=F32)

    def load(i):
        pair = pl.ds(2 * i, 2)
        return pltpu.make_async_copy(qd_hbm.at[pair], qd_ref.at[pair], qd_sem.at[i])

    for i in range(half):
        load(i).start()

    unit = eye(HD).astype(BF16)
    gain_cols = [
        jnp.sum(eye(HD) * gain_ref[layer : layer + 1, :], axis=1, keepdims=True)
        for layer in range(layers)
    ]

    for side, ref in enumerate((low_kv_ref, own_kv_ref)):
        for b in range(half):
            at = side * half + b
            for j in range(2):
                part = slice(j * rows, (j + 1) * rows)
                k_all[at, part, :] = ref[2 * b + j, :rows, :]
                v_all[at, part, :] = ref[2 * b + j, rows : 2 * rows, :]
            kt_all[:, at * size : (at + 1) * size] = dot(unit, k_all[at], NT).astype(BF16)

    ids_own = jnp.concatenate(
        [own_kv_ref[b, 2 * rows :, :][:1].astype(F32) for b in range(blocks)], 0
    )
    ids_low = jnp.concatenate(
        [low_kv_ref[b, 2 * rows :, :][:1].astype(F32) for b in range(blocks)], 0
    )
    begin = jnp.zeros((blocks, rows), F32)
    for doc in range(8):
        below = jnp.sum((ids_own < doc).astype(F32), keepdims=True)
        below_low = jnp.sum((ids_low < doc).astype(F32), keepdims=True)
        total = below + jnp.where(upper, below_low, float(blocks * rows))
        begin = jnp.where(ids_own == doc, total, begin)
    for b in range(half):
        start_all[b] = jnp.concatenate([begin[2 * b : 2 * b + 1], begin[2 * b + 1 : 2 * b + 2]], 1)
        first_all[b] = jnp.min(begin[2 * b : 2 * b + 1]).astype(jnp.int32) // size

    acc_k[...] = jnp.zeros_like(acc_k)
    acc_v[...] = jnp.zeros_like(acc_v)
    gain_acc[...] = jnp.zeros_like(gain_acc)

    def part_of(i, layer, h, offset):
        cols = slice(h * HD, (h + 1) * HD)
        return jnp.concatenate(
            [qd_ref[2 * i + j, offset + layer, :, cols] for j in range(2)], 0
        )

    def q_block(i, carry):
        load(i).wait()
        q_all = jnp.concatenate([part_of(i, layer, h, 0) for _, h, layer in chunks], 0)
        q_all = q_all.astype(F32).T
        for at, h, layer in chunks:
            q = q_all[:, at]
            inv = lax.rsqrt(jnp.mean(q * q, axis=0, keepdims=True) + 1e-6)
            qhat = q * inv
            inv_row[:, at] = inv
            qhat_t[:, at] = qhat
            normed_t[:, at] = (qhat * gain_cols[layer]).astype(BF16)
            dout[at, :] = part_of(i, layer, h, layers)
        begin_row = start_all[i]
        first = first_all[i]
        last = half + i
        count = last - first + 1
        begin_int = begin_row.astype(jnp.int32)
        token = last * size + lax.broadcasted_iota(jnp.int32, (1, size), 1)

        def sums(j, n, carry):
            kb = first + j
            k, v = k_all[kb], v_all[kb]
            u = kb * size + lax.broadcasted_iota(jnp.int32, (size, size), 0)
            allowed = u >= begin_int
            if j == n - 1:
                allowed = allowed & (u <= token)
            bias = jnp.where(allowed, 0.0, -1e30)
            out = []
            for (at, _, _), (top, total, weighted) in zip(chunks, carry):
                s = dot(k, normed_t[:, at], NN) + bias
                dp = dot(v, dout[at, :], NT)
                new = jnp.maximum(top, jnp.max(s, axis=0, keepdims=True))
                e = jnp.exp2((s - new) * rate)
                keep = jnp.exp2((top - new) * rate)
                expo[j, :, at] = e
                dprob[j, :, at] = dp
                tops[j, :, at] = new
                out.append(
                    (
                        new,
                        total * keep + jnp.sum(e, axis=0, keepdims=True),
                        weighted * keep + jnp.sum(e * dp, axis=0, keepdims=True),
                    )
                )
            return tuple(out)

        zero = jnp.zeros((1, size), F32)
        low = jnp.full((1, size), -1e30, F32)
        def run(n):
            stats = ((low, zero, zero),) * len(chunks)
            for j in range(n):
                stats = sums(j, n, stats)
            shares = [1.0 / total for _, total, _ in stats]
            deltas = [weighted * share for (_, _, weighted), share in zip(stats, shares)]

            def grads(j, carry):
                kb = first + j
                probs, scores = [], []
                for (at, _, _), (top, _, _), share, delta in zip(chunks, stats, shares, deltas):
                    prob = expo[j, :, at] * (share * jnp.exp2((tops[j, :, at] - top) * rate))
                    ds = (prob * ((dprob[j, :, at] - delta) * scale)).astype(BF16)
                    probs.append(prob.astype(BF16))
                    scores.append(ds)
                ds = jnp.concatenate(scores, 1)
                dscore[j * size : (j + 1) * size, :] = ds
                acc_k[kb] += dot(ds, normed_t[...], NT)
                acc_v[kb] += dot(jnp.concatenate(probs, 1), dout[...], NN)
                return carry

            for j in range(n):
                grads(j, 0)
            cols = pl.ds(pl.multiple_of(first * size, size), n * size)
            dq_t[...] = dot(kt_all[:, cols], dscore[: n * size, :], NN)

        for n in range(1, half + 2):
            pl.when(count == n)(functools.partial(run, n))

        for at, h, layer in chunks:
            dnorm, qhat = dq_t[:, at], qhat_t[:, at]
            part = dnorm * qhat
            gain_acc[layer] += part[:, :rows] + part[:, rows:]
            g = dnorm * gain_cols[layer]
            dq = inv_row[:, at] * (g - qhat * jnp.mean(g * qhat, axis=0, keepdims=True))
            dq = dq.T.astype(BF16)
            cols = slice(h * HD, (h + 1) * HD)
            for j in range(2):
                dq_out[2 * i + j, layer, :, cols] = dq[j * rows : (j + 1) * rows]
        pair = pl.ds(2 * i, 2)
        pltpu.make_async_copy(dq_out.at[pair], dq_ref.at[pair], sem.at[i]).start()
        return carry

    lax.fori_loop(0, half, q_block, 0)

    dgain_ref[...] = jnp.zeros_like(dgain_ref)
    for layer in range(layers):
        dgain_ref[layer : layer + 1, :] = jnp.sum(gain_acc[layer].T, axis=0, keepdims=True)
    copies = []
    for b in range(half):
        for j in range(2):
            part = slice(j * rows, (j + 1) * rows)
            for kv, acc in enumerate((acc_k, acc_v)):
                out = slice(kv * rows, (kv + 1) * rows)
                cross_out[2 * b + j, out, :] = acc[b, part, :].astype(BF16)
                own_out[2 * b + j, out, :] = acc[half + b, part, :]
        pair = pl.ds(2 * b, 2)
        for n, (src, dst) in enumerate(((cross_out, cross_ref), (own_out, own_ref))):
            copy = pltpu.make_async_copy(src.at[pair], dst.at[pair], sem.at[half * (n + 1) + b])
            copy.start()
            copies.append(copy)
    for b in range(half):
        pair = pl.ds(2 * b, 2)
        pltpu.make_async_copy(dq_out.at[pair], dq_ref.at[pair], sem.at[b]).wait()
    for copy in copies:
        copy.wait()


def attention(upper, kv_own, kv_low, qd, gain):
    parts, twice, rows, width = qd.shape
    layers = twice // 2
    kv_width = kv_own.shape[2]
    half = parts // 2
    size = 2 * rows
    stack = layers * (width // HD) * size
    return pl.pallas_call(
        attention_kernel,
        out_shape=(
            jax.ShapeDtypeStruct((parts, layers, rows, width), BF16),
            jax.ShapeDtypeStruct((parts, 2 * rows, kv_width), F32),
            jax.ShapeDtypeStruct((parts, 2 * rows, kv_width), BF16),
            jax.ShapeDtypeStruct((8, HD), F32),
        ),
        in_specs=[pl.BlockSpec(memory_space=pltpu.SMEM), whole(), whole(), in_hbm(), whole()],
        out_specs=(in_hbm(),) * 3 + (whole(),),
        scratch_shapes=[
            pltpu.VMEM((2 * half, size, HD), BF16),
            pltpu.VMEM((2 * half, size, HD), BF16),
            pltpu.VMEM((HD, 2 * half * size), BF16),
            pltpu.VMEM((half, 1, size), F32),
            pltpu.VMEM((HD, stack), F32),
            pltpu.VMEM((1, stack), F32),
            pltpu.VMEM((HD, stack), BF16),
            pltpu.VMEM((stack, HD), BF16),
            pltpu.VMEM((half + 1, size, stack), F32),
            pltpu.VMEM((half + 1, size, stack), F32),
            pltpu.VMEM((half + 1, 1, stack), F32),
            pltpu.VMEM((2 * half, size, HD), F32),
            pltpu.VMEM((2 * half, size, HD), F32),
            pltpu.VMEM((HD, stack), F32),
            pltpu.VMEM((layers, HD, rows), F32),
            pltpu.SMEM((half,), jnp.int32),
            pltpu.VMEM(((half + 1) * size, stack), BF16),
            pltpu.VMEM((parts, twice, rows, width), BF16),
            pltpu.SemaphoreType.DMA((half,)),
            pltpu.VMEM((parts, layers, rows, width), BF16),
            pltpu.VMEM((parts, 2 * rows, kv_width), F32),
            pltpu.VMEM((parts, 2 * rows, kv_width), BF16),
            pltpu.SemaphoreType.DMA((3 * half,)),
        ],
        compiler_params=params(52),
        name="attention",
    )(upper, kv_own, kv_low, qd, gain)


RING = 4


def pair_sum(x, axis, perm):
    return x + lax.ppermute(x, axis, perm)


def ring_sum(x, axis, shift):
    one, two, three = (lax.ppermute(x, axis, shift(k)) for k in (1, 2, 3))
    return (x + two) + (one + three)


def over_x(x):
    return ring_sum(
        x,
        "dp",
        lambda k: [
            (d, d // RING * RING + (d + k) % RING) for d in range(lax.axis_size("dp"))
        ],
    )


def over_z(x):
    n_sp, n_dp = lax.axis_size("sp"), lax.axis_size("dp")
    x = ring_sum(x, "dp", lambda k: [(d, (d + k * RING) % n_dp) for d in range(n_dp)])
    return pair_sum(x, "sp", [(s, (s + n_sp // 2) % n_sp) for s in range(n_sp)])


def on_device(queries, dout, keys, values, gain, segments):
    layers, _, rows, channels = queries.shape
    n_sp = lax.axis_size("sp")
    parts = n_sp // 2
    groups = [list(range(parts)), list(range(parts, n_sp))]
    low_to_up = [(s, s + parts) for s in range(parts)]
    up_to_low = [(s + parts, s) for s in range(parts)]
    width = channels // parts
    kv_width = keys.shape[2] // parts
    upper = (lax.axis_index("sp") >= parts).astype(jnp.int32).reshape(1)

    def exchange(x):
        return lax.all_to_all(x, "sp", 0, 0, axis_index_groups=groups, tiled=True)

    kv_send = pl.pallas_call(
        pack_kv_kernel,
        out_shape=jax.ShapeDtypeStruct((parts, 2 * rows + IDS, kv_width), BF16),
        in_specs=[whole()] * 3,
        out_specs=whole(),
        compiler_params=params(63),
        name="pack_kv",
    )(keys[0], values[0], segments)
    kv_own = exchange(kv_send)
    queries, dout, _ = lax.optimization_barrier((queries, dout, kv_send))
    qd_send = pl.pallas_call(
        pack_q_kernel,
        out_shape=jax.ShapeDtypeStruct((parts, 2 * layers, rows, width), BF16),
        in_specs=[whole()] * 2,
        out_specs=whole(),
        compiler_params=params(63),
        name="pack_q",
    )(queries[:, 0], dout[:, 0])
    kv_low = lax.ppermute(kv_own, "sp", low_to_up)
    qd = exchange(qd_send)

    dq_send, kv_sum, cross, dgain = attention(upper, kv_own, kv_low, qd, gain)

    cross_low = lax.ppermute(cross, "sp", up_to_low)
    dgain = over_x(dgain)
    dq_recv = exchange(dq_send)
    dgain = over_z(dgain)
    kv_out = pl.pallas_call(
        combine_kernel,
        out_shape=jax.ShapeDtypeStruct(
            (parts, 2 * rows + (PIECES + 1) * GAIN_ROWS, kv_width), BF16
        ),
        in_specs=[whole()] * 3,
        out_specs=whole(),
        compiler_params=params(16),
        name="combine",
    )(kv_sum, cross_low, dgain)
    dkv_recv = exchange(kv_out)
    dqueries = pl.pallas_call(
        unpack_q_kernel,
        out_shape=jax.ShapeDtypeStruct((layers, rows, channels), BF16),
        in_specs=[whole()],
        out_specs=whole(),
        compiler_params=params(16),
        name="unpack_q",
    )(dq_recv)
    dkeys, dvalues, dgain = pl.pallas_call(
        unpack_kv_kernel,
        out_shape=(jax.ShapeDtypeStruct((rows, keys.shape[2]), BF16),) * 2
        + (jax.ShapeDtypeStruct(gain.shape, F32),),
        in_specs=[whole()],
        out_specs=(whole(),) * 3,
        compiler_params=params(16),
        name="unpack_kv",
    )(dkv_recv)
    return dqueries[:, None], dkeys[None], dvalues[None], dgain


def solution(mesh):
    return jax.shard_map(
        on_device,
        mesh=mesh,
        in_specs=(
            P(None, "dp", "sp", None),
            P(None, "dp", "sp", None),
            P("dp", "sp", None),
            P("dp", "sp", None),
            P(),
            P("dp", "sp"),
        ),
        out_specs=(P(None, "dp", "sp", None), P("dp", "sp", None), P("dp", "sp", None), P()),
        check_vma=False,
    )
```
